256 devices in a mesh: sample: 16 (over x_lo, y, core), seq: 16 (over z, x_hi).
Axes of the slice: x: 4 (x_hi: 2, x_lo: 2; x = x_hi * 2 + x_lo), y: 4, z: 8, core: 2. Of those that a mesh axis runs over, the one named last changes fastest.
Arguments:
- atom_feats: bfloat16 [32, 16384, 128], P('sample', 'seq'), may hold values from -6 to 6
- atom_token: int32 [16384], P('seq'), may hold values from 0 to 2047, as said below
- single_cond: bfloat16 [32, 2048, 384], P('sample', 'seq'), may hold values from -6 to 6
- pair_rep: bfloat16 [2048, 2048, 128], P('seq', 'sample'), may hold values from -6 to 6
- w_atom: bfloat16 [128, 768], replicated, may hold values from -0.5 to 0.5
- w_ada_gate: bfloat16 [384, 768], replicated, may hold values from -0.3125 to 0.3125
- w_ada_shift: bfloat16 [384, 768], replicated, may hold values from -0.3125 to 0.3125
- w_query: bfloat16 [768, 768], replicated, may hold values from -1 to 1
- w_key: bfloat16 [768, 768], replicated, may hold values from -32 to 32
- w_value: bfloat16 [768, 768], replicated, may hold values from -0.21875 to 0.21875
- w_pair: bfloat16 [128, 16], replicated, may hold values from -1 to 1
- w_out: bfloat16 [768, 768], replicated, may hold values from -0.875 to 0.875
- w_outgate: bfloat16 [384, 768], replicated, may hold values from -0.3125 to 0.3125
- outgate_bias: bfloat16 [768], replicated, may hold values from -6 to 6
Outputs:
- update: bfloat16 [32, 2048, 768], P('sample', 'seq')
The draws below stay inside these ranges and needn't reach their ends.
Inputs may be any that keep to these rules, and one draw needn't show every extreme that they name: `atom_token`: sorted; every token has at least one atom; the atoms of one index p of seq belong to tokens of index p of seq and of index p + 1.
All inputs are finite; a program needn't handle non-finite values.
Results may differ from the reference program's by a relative error of at most 0.012.
The reference program's roundings to bfloat16 on the way count: a program that leaves them out, or rounds other values in their place, can miss the bound.
Values may be sent and summed in bfloat16 or wider, within the bound.
No kernel may reach another device: no remote copies, remote signals or barrier semaphores. Data moves between devices by JAX's collectives and lax.ppermute only.
A program may use at most 128 MiB of HBM per device.

```python
import math
import jax
import jax.numpy as jnp
from jax import lax

D = 768
HEADS = 16
HD = 48
CS = 384
CZ = 128
CA = 128
TOK_DEV = 128
ATOM_DEV = 1024
N = 2048
NA = 16384
SAMPLES = 32


def token_map(key):
    key = jax.random.fold_in(key, 11)
    block_count = N // TOK_DEV
    magnitude_key = jax.random.fold_in(key, 1)
    weight_key = jax.random.fold_in(key, 3)
    position = jnp.arange(block_count + 1, dtype=jnp.int32)
    magnitude = jax.random.randint(magnitude_key, (block_count + 1,), ATOM_DEV // 8, ATOM_DEV // 2 - TOK_DEV + 1)
    drifts = jnp.where((position == 0) | (position == block_count), 0, -magnitude)
    starts = position * ATOM_DEV + drifts
    block_sizes = starts[1:] - starts[:-1]
    weights = jax.random.randint(weight_key, (block_count, TOK_DEV), 1, 9)
    before = jnp.cumsum(weights, axis=1) - weights
    totals = jnp.sum(weights, axis=1, keepdims=True)
    spare_atoms = (block_sizes - TOK_DEV)[:, None]
    local_start = jnp.arange(TOK_DEV, dtype=jnp.int32)[None, :] + spare_atoms * before // totals
    token_start = (starts[:-1, None] + local_start).reshape(-1)
    atom_ids = jnp.arange(NA, dtype=jnp.int32)
    return (jnp.searchsorted(token_start, atom_ids, side='right') - 1).astype(jnp.int32)


def draw_atom_token(key, part):
    return token_map(key)


def draw_atom_feats(key, part):
    key = jax.random.fold_in(key, 31)
    noise = jax.random.normal(key, (SAMPLES, NA, CA), jnp.float32)
    return jnp.clip(noise, -6.0, 6.0).astype(jnp.bfloat16)


def draw_single_cond(key, part):
    key = jax.random.fold_in(key, 41)
    noise = jax.random.normal(key, (SAMPLES, N, CS), jnp.float32)
    return jnp.clip(noise, -6.0, 6.0).astype(jnp.bfloat16)


def query_key(key):
    scaling = D ** (-0.5)
    first = jax.random.normal(jax.random.fold_in(key, 51), (D, D), jnp.float32)
    second = jax.random.normal(jax.random.fold_in(key, 52), (D, D), jnp.float32)
    return (jnp.clip(first, -6.0, 6.0) * scaling, jnp.clip(second, -6.0, 6.0) * scaling)


def draw_w_query(key, part):
    first, second = query_key(key)
    return first.astype(jnp.bfloat16)


def draw_w_key(key, part):
    first, second = query_key(key)
    return second.astype(jnp.bfloat16)


def block_levels(key, extent, shards, low, high):
    def one(dim, blocks):
        heights = jax.random.uniform(jax.random.fold_in(jax.random.fold_in(key, 6), dim), (blocks,), jnp.float32, low / len(shards), high / len(shards))
        return jnp.repeat(jnp.exp(heights), extent[dim] // blocks).reshape((-1,) + (1,) * (len(extent) - dim - 1))

    loudness = one(*shards[0])
    for cut in shards[1:]:
        loudness = loudness * one(*cut)
    return loudness


def normal_values(key, shape, width, bound, split=(), held_as=jnp.bfloat16):
    entries = jax.random.normal(key, shape, jnp.float32) * width
    if len(split) > 0:
        entries = block_levels(key, shape, split, -0.22, 0.18) * entries
    return jnp.clip(entries, min=-bound, max=bound).astype(held_as)


def setup_inputs(seed: int = 0) -> dict:
    keys = jax.random.split(jax.random.key(seed), 15)
    return {
        "atom_feats": draw_atom_feats(jax.random.fold_in(keys[14], 71), 0),
        "atom_token": draw_atom_token(jax.random.fold_in(keys[14], 71), 0),
        "single_cond": draw_single_cond(jax.random.fold_in(keys[14], 71), 0),
        "pair_rep": normal_values(keys[3], (N, N, CZ), 1.0, 6.0, ((0, 16), (1, 16))),
        "w_atom": normal_values(keys[4], (CA, D), CA ** -0.5, 0.5),
        "w_ada_gate": normal_values(keys[5], (CS, D), CS ** -0.5, 0.3125),
        "w_ada_shift": normal_values(keys[6], (CS, D), CS ** -0.5, 0.3125),
        "w_query": draw_w_query(jax.random.fold_in(keys[14], 71), 0),
        "w_key": draw_w_key(jax.random.fold_in(keys[14], 71), 0),
        "w_value": normal_values(keys[9], (D, D), D ** -0.5, 0.21875),
        "w_pair": normal_values(keys[10], (CZ, HEADS), 0.18, 1.0),
        "w_out": normal_values(keys[11], (D, D), (D // 16) ** -0.5, 0.875),
        "w_outgate": normal_values(keys[12], (CS, D), CS ** -0.5, 0.3125),
        "outgate_bias": normal_values(keys[13], (D,), 1.5, 6.0),
    }


def layer_norm(inputs):
    average = lax.optimization_barrier(jnp.mean(inputs, axis=-1, keepdims=True))
    centered = inputs - average
    variance = lax.optimization_barrier(jnp.mean(centered * centered, axis=-1, keepdims=True))
    return centered * lax.rsqrt(variance + 1e-05)

def reference(atom_feats, atom_token, single_cond, pair_rep, w_atom, w_ada_gate, w_ada_shift, w_query, w_key, w_value, w_pair, w_out, w_outgate, outgate_bias):
    row_blocks = pair_rep.reshape(N // TOK_DEV, TOK_DEV, N, CZ)

    def bias_block(pair_rows):
        normed_pair = layer_norm(pair_rows.astype(jnp.float32)).astype(jnp.bfloat16)
        return jnp.einsum('ijc,ch->hij', normed_pair.astype(jnp.float32), w_pair.astype(jnp.float32)).astype(jnp.bfloat16)
    pair_bias = lax.map(bias_block, row_blocks)
    pair_bias = jnp.transpose(pair_bias, (1, 0, 2, 3)).reshape(HEADS, N, N)
    device_count = NA // ATOM_DEV
    owner_rows = jnp.arange(NA, dtype=jnp.int32) // ATOM_DEV
    segment_ids = (atom_token + owner_rows * N).astype(jnp.int32)
    atom_count = jax.ops.segment_sum(jnp.ones((NA,), jnp.float32), atom_token, num_segments=N)
    scaling = 1.0 / math.sqrt(HD)

    def one_sample(inputs):
        features, single = inputs
        hidden = jax.nn.relu(jnp.dot(features, w_atom, preferred_element_type=jnp.float32)).astype(jnp.bfloat16)
        partial_value = jax.ops.segment_sum(hidden.astype(jnp.float32), segment_ids, num_segments=device_count * N)
        partial_value = lax.optimization_barrier(partial_value.astype(jnp.bfloat16)).astype(jnp.float32)
        summed = lax.optimization_barrier(jnp.sum(partial_value.reshape(device_count, N, D), axis=0))
        tokens = summed / atom_count[:, None]
        cond = layer_norm(single.astype(jnp.float32)).astype(jnp.bfloat16)
        gate_ada = jax.nn.sigmoid(jnp.dot(cond, w_ada_gate, preferred_element_type=jnp.float32))
        shift_ada = jnp.dot(cond, w_ada_shift, preferred_element_type=jnp.float32)
        normed = (gate_ada * layer_norm(tokens) + shift_ada).astype(jnp.bfloat16)
        queries = jnp.dot(normed, w_query, preferred_element_type=jnp.float32).astype(jnp.bfloat16).reshape(N, HEADS, HD)
        key_heads = jnp.dot(normed, w_key, preferred_element_type=jnp.float32).astype(jnp.bfloat16).reshape(N, HEADS, HD)
        value_heads = jnp.dot(normed, w_value, preferred_element_type=jnp.float32).astype(jnp.bfloat16).reshape(N, HEADS, HD)

        def attend(offset):
            query_rows = lax.dynamic_slice_in_dim(queries, offset, TOK_DEV, 0)
            bias_slab = lax.dynamic_slice_in_dim(pair_bias, offset, TOK_DEV, 1)
            scores = jnp.einsum('qhd,khd->hqk', query_rows.astype(jnp.float32), key_heads.astype(jnp.float32)) * scaling + bias_slab.astype(jnp.float32)
            largest = lax.optimization_barrier(jnp.max(scores, axis=-1, keepdims=True))
            exponent = jnp.exp(scores - largest)
            weights = (exponent / lax.optimization_barrier(jnp.sum(exponent, axis=-1, keepdims=True))).astype(jnp.bfloat16)
            attended = jnp.einsum('hqk,khd->qhd', weights.astype(jnp.float32), value_heads.astype(jnp.float32)).astype(jnp.bfloat16)
            return attended.reshape(TOK_DEV, D)
        offsets = jnp.arange(N // TOK_DEV, dtype=jnp.int32) * TOK_DEV
        attended_all = lax.map(attend, offsets).reshape(N, D)
        out_gate = jax.nn.sigmoid(jnp.dot(cond, w_outgate, preferred_element_type=jnp.float32) + outgate_bias.astype(jnp.float32))
        mixed_out = jnp.dot(attended_all, w_out, preferred_element_type=jnp.float32)
        return (out_gate * mixed_out).astype(jnp.bfloat16)
    return lax.map(one_sample, (atom_feats, single_cond))
```

```python
import math

import jax
import jax.numpy as jnp
from jax import lax
from jax.experimental import pallas as pl
from jax.experimental.pallas import tpu as pltpu
from jax.sharding import PartitionSpec as P

F32 = jnp.float32
BF16 = jnp.bfloat16
LOG2E = 1.4426950408889634
ROWS = 256


def from_behind(value, axis, steps):
    count = lax.axis_size(axis)
    initial, last = (max(0, -steps), min(count, count - steps))
    return lax.ppermute(value, axis, [(source, source + steps) for source in range(initial, last)])


def layer_norm(inputs):
    average = jnp.mean(inputs, axis=-1, keepdims=True)
    centered = inputs - average
    variance = jnp.mean(centered * centered, axis=-1, keepdims=True)
    return centered * lax.rsqrt(variance + 1e-05)


def swap_core(value):
    return lax.ppermute(value, "sample", [(i, i ^ 1) for i in range(16)])


def swap_x(value):
    return lax.ppermute(value, "sample", [(i, i ^ 8) for i in range(16)])


def shift_y(value, steps):
    return lax.ppermute(
        value, "sample", [(i, (i & 9) | ((((i >> 1) + steps) & 3) << 1)) for i in range(16)]
    )


def attention_kernel(order_ref, kv_ref, *refs):
    pieces, (out_ref, q_scr, k_scr, v_scr, b_scr) = refs[:16], refs[16:]
    step = pl.program_id(0)
    blocks = kv_ref.shape[0]
    size = kv_ref.shape[1] // 3
    tok = kv_ref.shape[2] // 2
    scale = LOG2E / math.sqrt(size)

    @pl.when(step == 0)
    def _():
        for sample in range(2):
            lanes = slice(sample * tok, (sample + 1) * tok)
            for place in range(blocks):
                block = order_ref[place]
                q_scr[sample, place * tok : (place + 1) * tok, :] = (
                    kv_ref[place, :size, lanes].astype(F32).T.astype(BF16)
                )
                k_scr[sample, :, place * tok : (place + 1) * tok] = kv_ref[block, size : 2 * size, lanes]
                values = kv_ref[block, 2 * size :, lanes].astype(F32)
                padded = jnp.concatenate([values, jnp.ones((tok - size, tok), F32)], axis=0)
                v_scr[sample, place * tok : (place + 1) * tok, :] = padded.T.astype(BF16)

    for place in range(blocks):
        b_scr[:, place * tok : (place + 1) * tok] = pieces[place][...].astype(F32) * LOG2E

    row = pl.multiple_of(step * ROWS, ROWS)
    for sample in range(2):
        scores = jnp.dot(q_scr[sample, pl.ds(row, ROWS), :], k_scr[sample], preferred_element_type=F32)
        scores = scores * scale + b_scr[...]
        largest = jnp.max(scores, axis=-1, keepdims=True)
        weights = jnp.exp2(scores - largest).astype(BF16)
        mixed = jnp.dot(weights, v_scr[sample], preferred_element_type=F32)
        mixed = (mixed / mixed[:, size : size + 1]).T
        for part in range(ROWS // tok):
            out_ref[part, :, sample * tok : (sample + 1) * tok] = mixed[
                :size, part * tok : (part + 1) * tok
            ].astype(BF16)


def attention(order, kv, pieces):
    blocks, rows3, width = kv.shape
    size = rows3 // 3
    tok = width // 2
    total = blocks * tok
    return pl.pallas_call(
        attention_kernel,
        grid=(total // ROWS,),
        in_specs=[
            pl.BlockSpec(memory_space=pltpu.SMEM),
            pl.BlockSpec((blocks, rows3, width), lambda i: (0, 0, 0)),
        ]
        + [pl.BlockSpec((ROWS, tok), lambda i: (i, 0))] * blocks,
        out_specs=pl.BlockSpec((ROWS // tok, size, width), lambda i: (i, 0, 0)),
        out_shape=jax.ShapeDtypeStruct((blocks, size, width), BF16),
        scratch_shapes=[
            pltpu.VMEM((2, total, size), BF16),
            pltpu.VMEM((2, size, total), BF16),
            pltpu.VMEM((2, total, tok), BF16),
            pltpu.VMEM((ROWS, total), F32),
        ],
        compiler_params=pltpu.CompilerParams(vmem_limit_bytes=50 * 1024 * 1024),
        cost_estimate=pl.CostEstimate(
            flops=8 * total * total * 64, bytes_accessed=12 * 1024 * 1024, transcendentals=2 * total * total
        ),
    )(order, kv, *pieces)


def per_device(
    atom_feats,
    atom_token,
    single_cond,
    pair_rep,
    w_atom,
    w_ada_gate,
    w_ada_shift,
    w_query,
    w_key,
    w_value,
    w_pair,
    w_out,
    w_outgate,
    outgate_bias,
):
    samp_local = atom_feats.shape[0]
    atom_local = atom_feats.shape[1]
    tok_local = single_cond.shape[1]
    model_width = w_query.shape[1]
    head_count = w_pair.shape[1]
    head_size = model_width // head_count
    seq_place = lax.axis_index("seq")
    sample_place = lax.axis_index("sample")

    normed_pair = layer_norm(pair_rep.astype(F32)).astype(BF16)
    bias_local = jnp.einsum("ijc,ch->hij", normed_pair, w_pair, preferred_element_type=F32).astype(BF16)
    bias_own = lax.all_to_all(bias_local, "seq", 0, 0, tiled=True).reshape(-1, tok_local)

    hidden = jax.nn.relu(
        jnp.einsum("sac,cd->sad", atom_feats, w_atom, preferred_element_type=F32)
    ).astype(BF16)
    relative = atom_token - seq_place * tok_local
    slot_ids = lax.broadcasted_iota(jnp.int32, (2 * tok_local, atom_local), 0)
    member = slot_ids == relative[None, :]
    partial_value = jnp.einsum("ta,sad->std", member.astype(BF16), hidden, preferred_element_type=F32)
    counts = jnp.sum(member.astype(F32), axis=1)[None, :]
    rounded = partial_value.astype(BF16)
    count_sent = counts
    below_part, below_count = from_behind(
        (rounded[:, tok_local:], count_sent[:, tok_local:]), "seq", 1
    )
    summed = rounded[:, :tok_local].astype(F32) + below_part.astype(F32)
    token_counts = counts[:, :tok_local] + below_count
    tokens = summed / token_counts[:, :, None]
    cond = layer_norm(single_cond.astype(F32)).astype(BF16)
    gate_ada = jax.nn.sigmoid(jnp.einsum("stc,cd->std", cond, w_ada_gate, preferred_element_type=F32))
    shift_ada = jnp.einsum("stc,cd->std", cond, w_ada_shift, preferred_element_type=F32)
    normed = (gate_ada * layer_norm(tokens) + shift_ada).astype(BF16)
    flat = normed.reshape(samp_local * tok_local, model_width)

    def heads_of(weight):
        out = jnp.dot(flat, weight, preferred_element_type=F32).astype(BF16)
        return out.T.reshape(head_count, head_size, samp_local * tok_local)

    sent = jnp.concatenate([heads_of(w_query), heads_of(w_key), heads_of(w_value)], axis=1)
    kv = lax.all_to_all(sent, "seq", 0, 0, tiled=True)

    half = bias_own.shape[0] // 2
    mine = bias_own
    across = swap_x(mine)

    def ring(piece):
        up, down = shift_y(piece, 1), shift_y(piece, -1)
        far = jnp.concatenate([shift_y(up[:half], 1), shift_y(down[half:], -1)], axis=0)
        return [piece, up, down, far]

    pieces = ring(mine) + ring(across)
    pieces = pieces + [swap_core(piece) for piece in pieces]
    x_lo, y, core = sample_place // 8, sample_place // 2 % 4, sample_place % 2
    order = jnp.stack(
        [
            (x_lo ^ dx) * 8 + ((y + dy) % 4) * 2 + (core ^ dc)
            for dc in (0, 1)
            for dx in (0, 1)
            for dy in (0, 3, 1, 2)
        ]
    ).astype(jnp.int32)

    attended = attention(order, kv, pieces)
    attended = lax.all_to_all(attended, "seq", 0, 0, tiled=True).reshape(model_width, -1)
    out_gate = jax.nn.sigmoid(
        jnp.einsum("std,de->ste", cond, w_outgate, preferred_element_type=F32)
        + outgate_bias.astype(F32)
    )
    mixed_out = jnp.einsum("dt,de->te", attended, w_out, preferred_element_type=F32)
    return (out_gate * mixed_out.reshape(out_gate.shape)).astype(BF16)


def solution(mesh):
    return jax.shard_map(
        per_device,
        mesh=mesh,
        in_specs=(
            P("sample", "seq", None),
            P("seq"),
            P("sample", "seq", None),
            P("seq", "sample", None),
            P(),
            P(),
            P(),
            P(),
            P(),
            P(),
            P(),
            P(),
            P(),
            P(),
        ),
        out_specs=P("sample", "seq", None),
        check_vma=False,
    )
```

```python
import math

import jax
import jax.numpy as jnp
from jax import lax
from jax.experimental import pallas as pl
from jax.experimental.pallas import tpu as pltpu
from jax.sharding import PartitionSpec as P

F32 = jnp.float32
BF16 = jnp.bfloat16
LOG2E = 1.4426950408889634
ROWS = 256


def from_behind(value, axis, steps):
    count = lax.axis_size(axis)
    initial, last = (max(0, -steps), min(count, count - steps))
    return lax.ppermute(value, axis, [(source, source + steps) for source in range(initial, last)])


def layer_norm(inputs):
    average = jnp.mean(inputs, axis=-1, keepdims=True)
    centered = inputs - average
    variance = jnp.mean(centered * centered, axis=-1, keepdims=True)
    return centered * lax.rsqrt(variance + 1e-05)


def swap_core(value):
    return lax.ppermute(value, "sample", [(i, i ^ 1) for i in range(16)])


def swap_x(value):
    return lax.ppermute(value, "sample", [(i, i ^ 8) for i in range(16)])


def shift_y(value, steps):
    return lax.ppermute(
        value, "sample", [(i, (i & 9) | ((((i >> 1) + steps) & 3) << 1)) for i in range(16)]
    )


def pair_kernel(pair_ref, weight_ref, out_ref, sum_weights, square_weights, mean_weights, bias_scr):
    step = pl.program_id(0)
    groups, eight, keys, depth = pair_ref.shape
    heads = weight_ref.shape[0]
    width = heads * eight

    @pl.when(step == 0)
    def _():
        lane = lax.broadcasted_iota(jnp.int32, (heads, width), 1)
        row = lax.broadcasted_iota(jnp.int32, (heads, width), 0)
        spread = (lane // eight == row).astype(BF16)
        repeated = lax.dot_general(
            weight_ref[...], spread, (((0,), (0,)), ((), ())), preferred_element_type=F32
        )
        mean_weights[...] = jnp.broadcast_to(
            jnp.sum(repeated, axis=0, keepdims=True) * (1.0 / depth), mean_weights.shape
        )
        place = lax.broadcasted_iota(jnp.int32, (depth, width), 1) % eight
        for i in range(eight):
            own = place == i
            ones = jnp.where(own, 1.0, 0.0).astype(BF16)
            sum_weights[i * depth : (i + 1) * depth, :width] = jnp.where(own, repeated, 0.0).astype(BF16)
            sum_weights[i * depth : (i + 1) * depth, width:] = ones
            square_weights[2 * i * depth : (2 * i + 1) * depth, :] = ones
            square_weights[(2 * i + 1) * depth : (2 * i + 2) * depth, :] = ones

    rows = [pair_ref[:, i].reshape(groups * keys, depth) for i in range(eight)]
    sums = jnp.dot(jnp.concatenate(rows, axis=1), sum_weights[...], preferred_element_type=F32)
    parts = []
    for value in rows:
        wide = value.astype(F32)
        square = wide * wide
        high = square.astype(BF16)
        parts += [high, (square - high.astype(F32)).astype(BF16)]
    squares = jnp.dot(jnp.concatenate(parts, axis=1), square_weights[...], preferred_element_type=F32)
    total = sums[:, width:]
    mean = total * (1.0 / depth)
    variance = squares * (1.0 / depth) - mean * mean
    bias = (sums[:, :width] - total * mean_weights[0:1]) * lax.rsqrt(variance + 1e-05)
    for group in range(groups):
        turned = bias[group * keys : (group + 1) * keys].T
        for head in range(heads):
            bias_scr[head, pl.ds((step * groups + group) * eight, eight), :] = turned[
                head * eight : (head + 1) * eight
            ]

    @pl.when(step == pl.num_programs(0) - 1)
    def _():
        for head in range(heads):
            out_ref[head] = bias_scr[head].T.astype(BF16)


def pair_bias_local(pair_rep, w_pair, groups=8):
    queries, keys, depth = pair_rep.shape
    heads = w_pair.shape[1]
    eight = 8
    width = heads * eight
    return pl.pallas_call(
        pair_kernel,
        grid=(queries // (eight * groups),),
        in_specs=[
            pl.BlockSpec((groups, eight, keys, depth), lambda i: (i, 0, 0, 0)),
            pl.BlockSpec((heads, depth), lambda i: (0, 0)),
        ],
        out_specs=pl.BlockSpec((heads, keys, queries), lambda i: (0, 0, 0)),
        out_shape=jax.ShapeDtypeStruct((heads, keys, queries), BF16),
        scratch_shapes=[
            pltpu.VMEM((eight * depth, 2 * width), BF16),
            pltpu.VMEM((2 * eight * depth, width), BF16),
            pltpu.VMEM((8, width), F32),
            pltpu.VMEM((heads, queries, keys), F32),
        ],
        compiler_params=pltpu.CompilerParams(vmem_limit_bytes=40 * 1024 * 1024),
        cost_estimate=pl.CostEstimate(
            flops=2 * queries * keys * depth * 256, bytes_accessed=5 * 1024 * 1024, transcendentals=queries * keys
        ),
    )(pair_rep.reshape(queries // eight, eight, keys, depth), w_pair.T)


def attention_kernel(order_ref, kv_ref, *refs):
    count = len(refs) - 11
    pieces = refs[:count]
    out_ref, q_scr, k_scr, v_scr, b_scr, s_even, s_odd, m_even, m_odd, sems, kv_scr = refs[count:]
    scores_scr, top_scr = (s_even, s_odd), (m_even, m_odd)
    blocks, size, width = out_ref.shape
    tok = width // 2
    total = blocks * tok
    per_step = ROWS // tok
    steps = blocks // per_step
    chunk = 2 * tok
    scale = LOG2E / math.sqrt(size)

    def copies(step):
        found = []
        for place in range(blocks):
            five, kind = place // 4 * 5, place % 4
            start = step * per_step
            if kind == 3:
                found.append((pieces[five + 3 + start * 2 // blocks], start % (blocks // 2)))
            else:
                found.append((pieces[five + kind], start))
        return [
            pltpu.make_async_copy(
                piece.at[pl.ds(start, per_step)],
                b_scr.at[place, pl.ds(step * per_step, per_step)],
                sems.at[step, place],
            )
            for place, (piece, start) in enumerate(found)
        ]

    kv_copy = pltpu.make_async_copy(kv_ref, kv_scr, sems.at[steps, 0])
    kv_copy.start()
    for step in range(steps):
        for copy in copies(step):
            copy.start()
    kv_copy.wait()

    for sample in range(2):
        lanes = slice(sample * tok, (sample + 1) * tok)
        for place in range(blocks):
            block = order_ref[place]
            span = slice(place * tok, (place + 1) * tok)
            query = kv_scr[place, :size, lanes].astype(F32) * scale
            high = query.astype(BF16)
            q_scr[sample, :size, span] = high
            q_scr[sample, size:, span] = (query - high.astype(F32)).astype(BF16)
            key = kv_scr[block, size : 2 * size, lanes].astype(F32)
            k_scr[sample, span, :] = jnp.concatenate([key, key], axis=0).T.astype(BF16)
            v_scr[sample, :size, span] = kv_scr[block, 2 * size :, lanes]
            v_scr[sample, size:, span] = jnp.ones((v_scr.shape[1] - size, tok), BF16)

    def score(step, slot):
        held = {}

        def part(c):
            if c == 0:
                for place in range(blocks):
                    pltpu.make_async_copy(
                        pieces[0].at[pl.ds(0, per_step)],
                        b_scr.at[place, pl.ds(step * per_step, per_step)],
                        sems.at[step, place],
                    ).wait()
                column = step * ROWS if isinstance(step, int) else pl.multiple_of(step * ROWS, ROWS)
                held["q"] = [q_scr[sample, :, pl.ds(column, ROWS)] for sample in range(2)]
            span = slice(c * chunk, (c + 1) * chunk)
            bias = jnp.concatenate(
                [
                    jnp.concatenate([b_scr[place, step * per_step + t] for t in range(per_step)], axis=1)
                    for place in range(c * chunk // tok, (c + 1) * chunk // tok)
                ],
                axis=0,
            )
            bias = bias.astype(F32) * LOG2E
            for sample in range(2):
                scores = (
                    jnp.dot(k_scr[sample, span, :], held["q"][sample], preferred_element_type=F32) + bias
                )
                scores_scr[slot][sample, span, :] = scores
                top = scores.reshape(chunk // 8, 8, ROWS)
                while top.shape[0] > 4:
                    half = top.shape[0] // 2
                    top = jnp.maximum(top[:half], top[half:])
                held[sample] = top if c == 0 else jnp.maximum(held[sample], top)
                if c == total // chunk - 1:
                    top_scr[slot][sample] = jnp.max(held[sample], axis=0)

        return [lambda c=c: part(c) for c in range(total // chunk)]

    def weigh(step, slot):
        held = {}

        def part(c):
            span = slice(c * chunk, (c + 1) * chunk)
            for sample in range(2):
                if c == 0:
                    held[sample] = jnp.max(top_scr[slot][sample], axis=0, keepdims=True)
                weights = jnp.exp2(scores_scr[slot][sample, span, :] - held[sample]).astype(BF16)
                mixed = jnp.dot(v_scr[sample, :, span], weights, preferred_element_type=F32)
                mixed = mixed if c == 0 else held[sample, 0] + mixed
                held[sample, 0] = mixed
                if c == total // chunk - 1:
                    result = (mixed[:size] / mixed[size : size + 1]).astype(BF16)
                    for t in range(per_step):
                        out_ref[step * per_step + t, :, sample * tok : (sample + 1) * tok] = result[
                            :, t * tok : (t + 1) * tok
                        ]

        return [lambda c=c: part(c) for c in range(total // chunk)]

    def run(*lists):
        for together in zip(*lists):
            for work in together:
                work()

    run(score(0, 0))

    def body(pair, _):
        run(score(2 * pair + 1, 1), weigh(2 * pair, 0))
        run(score(2 * pair + 2, 0), weigh(2 * pair + 1, 1))
        return 0

    lax.fori_loop(0, steps // 2 - 1, body, 0)
    run(score(steps - 1, 1), weigh(steps - 2, 0))
    run(weigh(steps - 1, 1))


def attention(order, kv, pieces):
    blocks, rows3, width = kv.shape
    size = rows3 // 3
    tok = width // 2
    total = blocks * tok
    any_place = pl.BlockSpec(memory_space=pl.ANY)
    return pl.pallas_call(
        attention_kernel,
        in_specs=[pl.BlockSpec(memory_space=pltpu.SMEM), any_place] + [any_place] * len(pieces),
        out_specs=pl.BlockSpec(memory_space=pltpu.VMEM),
        out_shape=jax.ShapeDtypeStruct((blocks, size, width), BF16),
        scratch_shapes=[
            pltpu.VMEM((2, 2 * size, total), BF16),
            pltpu.VMEM((2, total, 2 * size), BF16),
            pltpu.VMEM((2, 64, total), BF16),
            pltpu.VMEM((blocks, blocks, tok, tok), BF16),
            pltpu.VMEM((2, total, ROWS), F32),
            pltpu.VMEM((2, total, ROWS), F32),
            pltpu.VMEM((2, 8, ROWS), F32),
            pltpu.VMEM((2, 8, ROWS), F32),
            pltpu.SemaphoreType.DMA((total // ROWS + 1, blocks)),
            pltpu.VMEM(kv.shape, BF16),
        ],
        compiler_params=pltpu.CompilerParams(vmem_limit_bytes=60 * 1024 * 1024),
        cost_estimate=pl.CostEstimate(
            flops=8 * total * total * 64, bytes_accessed=12 * 1024 * 1024, transcendentals=2 * total * total
        ),
    )(order, kv, *pieces)


def finish_kernel(attended_ref, weight_ref, gate_ref, out_ref):
    mixed = lax.dot_general(
        attended_ref[...], weight_ref[...], (((0,), (0,)), ((), ())), preferred_element_type=F32
    )
    out_ref[...] = (gate_ref[...] * mixed).astype(BF16)


def per_device(
    atom_feats,
    atom_token,
    single_cond,
    pair_rep,
    w_atom,
    w_ada_gate,
    w_ada_shift,
    w_query,
    w_key,
    w_value,
    w_pair,
    w_out,
    w_outgate,
    outgate_bias,
):
    samp_local = atom_feats.shape[0]
    atom_local = atom_feats.shape[1]
    tok_local = single_cond.shape[1]
    model_width = w_query.shape[1]
    head_count = w_pair.shape[1]
    head_size = model_width // head_count
    seq_place = lax.axis_index("seq")
    sample_place = lax.axis_index("sample")

    bias_local = pair_bias_local(pair_rep, w_pair)
    mine = lax.all_to_all(bias_local, "seq", 0, 0, tiled=True)

    hidden = jax.nn.relu(
        jnp.einsum("sac,cd->sad", atom_feats, w_atom, preferred_element_type=F32)
    ).astype(BF16)
    relative = atom_token - seq_place * tok_local
    slot_ids = lax.broadcasted_iota(jnp.int32, (2 * tok_local, atom_local), 0)
    member = slot_ids == relative[None, :]
    partial_value = jnp.einsum("ta,sad->std", member.astype(BF16), hidden, preferred_element_type=F32)
    counts = jnp.sum(member.astype(F32), axis=1)[None, :]
    rounded = partial_value.astype(BF16)
    below_part, below_count = from_behind(
        (rounded[:, tok_local:], counts[:, tok_local:]), "seq", 1
    )
    summed = rounded[:, :tok_local].astype(F32) + below_part.astype(F32)
    token_counts = counts[:, :tok_local] + below_count
    tokens = summed / token_counts[:, :, None]
    cond = layer_norm(single_cond.astype(F32)).astype(BF16)
    out_gate = jax.nn.sigmoid(
        jnp.einsum("std,de->ste", cond, w_outgate, preferred_element_type=F32)
        + outgate_bias.astype(F32)
    ).reshape(samp_local * tok_local, model_width)
    gate_ada = jax.nn.sigmoid(jnp.einsum("stc,cd->std", cond, w_ada_gate, preferred_element_type=F32))
    shift_ada = jnp.einsum("stc,cd->std", cond, w_ada_shift, preferred_element_type=F32)
    normed = (gate_ada * layer_norm(tokens) + shift_ada).astype(BF16)
    flat = normed.reshape(samp_local * tok_local, model_width)

    def heads_of(weight):
        out = jnp.dot(flat, weight, preferred_element_type=F32).astype(BF16)
        return out.T.reshape(head_count, head_size, samp_local * tok_local)

    sent = jnp.concatenate([heads_of(w_query), heads_of(w_key), heads_of(w_value)], axis=1)
    kv = lax.all_to_all(sent, "seq", 0, 0, tiled=True)

    half = mine.shape[0] // 2
    across = swap_x(mine)
    up, down = shift_y(mine, 1), shift_y(mine, -1)
    far = [shift_y(up[:half], 1), shift_y(down[half:], -1)]
    across_up, across_down = shift_y(across, 1), shift_y(across, -1)
    across_far = [swap_x(part) for part in far]
    pieces = [mine, up, down, *far, across, across_up, across_down, *across_far]
    pieces = pieces + [swap_core(piece) for piece in pieces]
    x_lo, y, core = sample_place // 8, sample_place // 2 % 4, sample_place % 2
    order = jnp.stack(
        [
            (x_lo ^ dx) * 8 + ((y + dy) % 4) * 2 + (core ^ dc)
            for dc in (0, 1)
            for dx in (0, 1)
            for dy in (0, 3, 1, 2)
        ]
    ).astype(jnp.int32)

    attended = attention(order, kv, pieces)
    attended = lax.all_to_all(attended, "seq", 0, 0, tiled=True).reshape(model_width, -1)
    out = pl.pallas_call(
        finish_kernel,
        out_shape=jax.ShapeDtypeStruct((samp_local * tok_local, model_width), BF16),
        compiler_params=pltpu.CompilerParams(vmem_limit_bytes=40 * 1024 * 1024),
    )(attended, w_out, out_gate)
    return out.reshape(samp_local, tok_local, model_width)


def solution(mesh):
    return jax.shard_map(
        per_device,
        mesh=mesh,
        in_specs=(
            P("sample", "seq", None),
            P("seq"),
            P("sample", "seq", None),
            P("seq", "sample", None),
            P(),
            P(),
            P(),
            P(),
            P(),
            P(),
            P(),
            P(),
            P(),
            P(),
        ),
        out_specs=P("sample", "seq", None),
        check_vma=False,
    )
```

```python
import math

import jax
import jax.numpy as jnp
from jax import lax
from jax.experimental import pallas as pl
from jax.experimental.pallas import tpu as pltpu
from jax.sharding import PartitionSpec as P

F32 = jnp.float32
BF16 = jnp.bfloat16
LOG2E = 1.4426950408889634
ROWS = 256


def from_behind(value, axis, steps):
    count = lax.axis_size(axis)
    initial, last = (max(0, -steps), min(count, count - steps))
    return lax.ppermute(value, axis, [(source, source + steps) for source in range(initial, last)])


def layer_norm(inputs):
    average = jnp.mean(inputs, axis=-1, keepdims=True)
    centered = inputs - average
    variance = jnp.mean(centered * centered, axis=-1, keepdims=True)
    return centered * lax.rsqrt(variance + 1e-05)


def swap_core(value):
    return lax.ppermute(value, "sample", [(i, i ^ 1) for i in range(16)])


def swap_x(value):
    return lax.ppermute(value, "sample", [(i, i ^ 8) for i in range(16)])


def shift_y(value, steps):
    return lax.ppermute(
        value, "sample", [(i, (i & 9) | ((((i >> 1) + steps) & 3) << 1)) for i in range(16)]
    )


def pair_kernel(pair_ref, weight_ref, out_ref, wide_weights, bias_scr):
    step = pl.program_id(0)
    groups, eight, keys, depth = pair_ref.shape
    heads = weight_ref.shape[0]
    width = heads * eight

    @pl.when(step == 0)
    def _():
        lane = lax.broadcasted_iota(jnp.int32, (heads, width), 1)
        row = lax.broadcasted_iota(jnp.int32, (heads, width), 0)
        spread = (lane // eight == row).astype(BF16)
        repeated = lax.dot_general(
            weight_ref[...], spread, (((0,), (0,)), ((), ())), preferred_element_type=F32
        )
        place = lax.broadcasted_iota(jnp.int32, (depth, width), 1) % eight
        for i in range(eight):
            wide_weights[i * depth : (i + 1) * depth, :] = jnp.where(place == i, repeated, 0.0).astype(BF16)

    ones = jnp.ones((depth, depth), BF16)
    normed = []
    for i in range(eight):
        value = pair_ref[:, i].reshape(groups * keys, depth)
        mean = jnp.dot(value, ones, preferred_element_type=F32) * (1.0 / depth)
        centered = value.astype(F32) - mean
        variance = jnp.mean(centered * centered, axis=-1, keepdims=True)
        normed.append((centered * lax.rsqrt(variance + 1e-05)).astype(BF16))
    bias = jnp.dot(jnp.concatenate(normed, axis=1), wide_weights[...], preferred_element_type=F32)
    for group in range(groups):
        turned = bias[group * keys : (group + 1) * keys].T
        for head in range(heads):
            bias_scr[head, pl.ds((step * groups + group) * eight, eight), :] = turned[
                head * eight : (head + 1) * eight
            ]

    @pl.when(step == pl.num_programs(0) - 1)
    def _():
        for head in range(heads):
            out_ref[head] = bias_scr[head].T.astype(BF16)


def pair_bias_local(pair_rep, w_pair, groups=8):
    queries, keys, depth = pair_rep.shape
    heads = w_pair.shape[1]
    eight = 8
    return pl.pallas_call(
        pair_kernel,
        grid=(queries // (eight * groups),),
        in_specs=[
            pl.BlockSpec((groups, eight, keys, depth), lambda i: (i, 0, 0, 0)),
            pl.BlockSpec((heads, depth), lambda i: (0, 0)),
        ],
        out_specs=pl.BlockSpec((heads, keys, queries), lambda i: (0, 0, 0)),
        out_shape=jax.ShapeDtypeStruct((heads, keys, queries), BF16),
        scratch_shapes=[
            pltpu.VMEM((eight * depth, heads * eight), BF16),
            pltpu.VMEM((heads, queries, keys), F32),
        ],
        compiler_params=pltpu.CompilerParams(vmem_limit_bytes=60 * 1024 * 1024),
        cost_estimate=pl.CostEstimate(
            flops=2 * queries * keys * depth * 256, bytes_accessed=5 * 1024 * 1024, transcendentals=queries * keys
        ),
    )(pair_rep.reshape(queries // eight, eight, keys, depth), w_pair.T)


def atom_kernel(feats_ref, relative_ref, weight_ref, own_ref, count_ref, sent_ref):
    samples, atoms, _ = feats_ref.shape
    tok, width = count_ref.shape[0], weight_ref.shape[1]
    slots = lax.broadcasted_iota(jnp.int32, (2 * tok, atoms), 0)
    member = jnp.where(slots == relative_ref[...], 1.0, 0.0)
    counts = jnp.sum(member, axis=1, keepdims=True)
    member = member.astype(BF16)
    count_ref[...] = jnp.broadcast_to(counts[:tok], count_ref.shape)
    above = jnp.broadcast_to(counts[tok:], count_ref.shape)
    high = jnp.floor(above * (1.0 / 256.0)) * 256.0
    lane = lax.broadcasted_iota(jnp.int32, count_ref.shape, 1)
    tail = jnp.where(lane == 0, high, jnp.where(lane == 1, above - high, 0.0)).astype(BF16)
    for sample in range(samples):
        hidden = jnp.dot(feats_ref[sample], weight_ref[...], preferred_element_type=F32)
        hidden = jnp.maximum(hidden, 0.0).astype(BF16)
        partial = jnp.dot(member, hidden, preferred_element_type=F32).astype(BF16)
        own_ref[sample] = partial[:tok]
        sent_ref[sample, :, :width] = partial[tok:]
        sent_ref[sample, :, width:] = tail


def token_kernel(own_ref, count_ref, came_ref, gate_ref, shift_ref, wq_ref, wk_ref, wv_ref, out_ref):
    samples, tok, width = own_ref.shape
    heads, size = out_ref.shape[0], out_ref.shape[1] // 3
    parts = []
    for sample in range(samples):
        tail = came_ref[sample, :, width:].astype(F32)
        count = count_ref[:, 0:1] + tail[:, 0:1] + tail[:, 1:2]
        summed = own_ref[sample].astype(F32) + came_ref[sample, :, :width].astype(F32)
        tokens = summed / count
        average = jnp.mean(tokens, axis=-1, keepdims=True)
        centered = tokens - average
        variance = jnp.mean(centered * centered, axis=-1, keepdims=True)
        normed = centered * lax.rsqrt(variance + 1e-05)
        parts.append((gate_ref[sample] * normed + shift_ref[sample]).astype(BF16))
    normed = jnp.concatenate(parts, axis=0)
    for kind, weight_ref in enumerate((wq_ref, wk_ref, wv_ref)):
        result = jnp.dot(normed, weight_ref[...], preferred_element_type=F32)
        turned = result.T.astype(BF16)
        for head in range(heads):
            out_ref[head, kind * size : (kind + 1) * size, :] = turned[head * size : (head + 1) * size]


def attention_kernel(order_ref, kv_ref, *refs):
    count = len(refs) - 11
    pieces = refs[:count]
    out_ref, q_scr, k_scr, v_scr, b_scr, s_even, s_odd, m_even, m_odd, sems, kv_scr = refs[count:]
    scores_scr, top_scr = (s_even, s_odd), (m_even, m_odd)
    blocks, size, width = out_ref.shape
    tok = width // 2
    total = blocks * tok
    per_step = ROWS // tok
    steps = blocks // per_step
    chunk = 2 * tok
    scale = LOG2E / math.sqrt(size)

    def copies(step):
        found = []
        for place in range(blocks):
            first, start = place + place // 8, step * per_step
            if place % 8 == 7:
                found.append((pieces[first + start * 2 // blocks], start % (blocks // 2)))
            else:
                found.append((pieces[first], start))
        return [
            pltpu.make_async_copy(
                piece.at[pl.ds(start, per_step)],
                b_scr.at[place, pl.ds(step * per_step, per_step)],
                sems.at[step, place],
            )
            for place, (piece, start) in enumerate(found)
        ]

    kv_copy = pltpu.make_async_copy(kv_ref, kv_scr, sems.at[steps, 0])
    kv_copy.start()
    for step in range(steps):
        for copy in copies(step):
            copy.start()
    kv_copy.wait()

    for sample in range(2):
        lanes = slice(sample * tok, (sample + 1) * tok)
        for place in range(blocks):
            block = order_ref[place]
            span = slice(place * tok, (place + 1) * tok)
            query = kv_scr[place, :size, lanes].astype(F32) * scale
            high = query.astype(BF16)
            q_scr[sample, :size, span] = high
            q_scr[sample, size:, span] = (query - high.astype(F32)).astype(BF16)
            key = kv_scr[block, size : 2 * size, lanes].astype(F32)
            k_scr[sample, span, :] = jnp.concatenate([key, key], axis=0).T.astype(BF16)
            v_scr[sample, :size, span] = kv_scr[block, 2 * size :, lanes]
            v_scr[sample, size:, span] = jnp.ones((v_scr.shape[1] - size, tok), BF16)

    def score(step, slot):
        held = {}

        def part(c):
            if c == 0:
                for place in range(blocks):
                    pltpu.make_async_copy(
                        pieces[0].at[pl.ds(0, per_step)],
                        b_scr.at[place, pl.ds(step * per_step, per_step)],
                        sems.at[step, place],
                    ).wait()
                column = step * ROWS if isinstance(step, int) else pl.multiple_of(step * ROWS, ROWS)
                held["q"] = [q_scr[sample, :, pl.ds(column, ROWS)] for sample in range(2)]
            span = slice(c * chunk, (c + 1) * chunk)
            bias = jnp.concatenate(
                [
                    jnp.concatenate([b_scr[place, step * per_step + t] for t in range(per_step)], axis=1)
                    for place in range(c * chunk // tok, (c + 1) * chunk // tok)
                ],
                axis=0,
            )
            bias = bias.astype(F32) * LOG2E
            for sample in range(2):
                scores = (
                    jnp.dot(k_scr[sample, span, :], held["q"][sample], preferred_element_type=F32) + bias
                )
                scores_scr[slot][sample, span, :] = scores
                top = scores.reshape(chunk // 8, 8, ROWS)
                while top.shape[0] > 4:
                    half = top.shape[0] // 2
                    top = jnp.maximum(top[:half], top[half:])
                held[sample] = top if c == 0 else jnp.maximum(held[sample], top)
                if c == total // chunk - 1:
                    top_scr[slot][sample] = jnp.max(held[sample], axis=0)

        return [lambda c=c: part(c) for c in range(total // chunk)]

    def weigh(step, slot):
        held = {}

        def part(c):
            span = slice(c * chunk, (c + 1) * chunk)
            for sample in range(2):
                if c == 0:
                    held[sample] = jnp.max(top_scr[slot][sample], axis=0, keepdims=True)
                weights = jnp.exp2(scores_scr[slot][sample, span, :] - held[sample]).astype(BF16)
                mixed = jnp.dot(v_scr[sample, :, span], weights, preferred_element_type=F32)
                mixed = mixed if c == 0 else held[sample, 0] + mixed
                held[sample, 0] = mixed
                if c == total // chunk - 1:
                    result = (mixed[:size] / mixed[size : size + 1]).astype(BF16)
                    for t in range(per_step):
                        out_ref[step * per_step + t, :, sample * tok : (sample + 1) * tok] = result[
                            :, t * tok : (t + 1) * tok
                        ]

        return [lambda c=c: part(c) for c in range(total // chunk)]

    def run(*lists):
        for together in zip(*lists):
            for work in together:
                work()

    run(score(0, 0))

    def body(pair, _):
        run(score(2 * pair + 1, 1), weigh(2 * pair, 0))
        run(score(2 * pair + 2, 0), weigh(2 * pair + 1, 1))
        return 0

    lax.fori_loop(0, steps // 2 - 1, body, 0)
    run(score(steps - 1, 1), weigh(steps - 2, 0))
    run(weigh(steps - 1, 1))


def attention(order, kv, pieces):
    blocks, rows3, width = kv.shape
    size = rows3 // 3
    tok = width // 2
    total = blocks * tok
    any_place = pl.BlockSpec(memory_space=pl.ANY)
    return pl.pallas_call(
        attention_kernel,
        in_specs=[pl.BlockSpec(memory_space=pltpu.SMEM), any_place] + [any_place] * len(pieces),
        out_specs=pl.BlockSpec(memory_space=pltpu.VMEM),
        out_shape=jax.ShapeDtypeStruct((blocks, size, width), BF16),
        scratch_shapes=[
            pltpu.VMEM((2, 2 * size, total), BF16),
            pltpu.VMEM((2, total, 2 * size), BF16),
            pltpu.VMEM((2, 64, total), BF16),
            pltpu.VMEM((blocks, blocks, tok, tok), BF16),
            pltpu.VMEM((2, total, ROWS), F32),
            pltpu.VMEM((2, total, ROWS), F32),
            pltpu.VMEM((2, 8, ROWS), F32),
            pltpu.VMEM((2, 8, ROWS), F32),
            pltpu.SemaphoreType.DMA((total // ROWS + 1, blocks)),
            pltpu.VMEM(kv.shape, BF16),
        ],
        compiler_params=pltpu.CompilerParams(vmem_limit_bytes=36 * 1024 * 1024),
        cost_estimate=pl.CostEstimate(
            flops=8 * total * total * 64, bytes_accessed=12 * 1024 * 1024, transcendentals=2 * total * total
        ),
    )(order, kv, *pieces)


def finish_kernel(attended_ref, weight_ref, gate_ref, out_ref):
    mixed = lax.dot_general(
        attended_ref[...], weight_ref[...], (((0,), (0,)), ((), ())), preferred_element_type=F32
    )
    out_ref[...] = (gate_ref[...] * mixed).astype(BF16)


def per_device(
    atom_feats,
    atom_token,
    single_cond,
    pair_rep,
    w_atom,
    w_ada_gate,
    w_ada_shift,
    w_query,
    w_key,
    w_value,
    w_pair,
    w_out,
    w_outgate,
    outgate_bias,
):
    samp_local = atom_feats.shape[0]
    atom_local = atom_feats.shape[1]
    tok_local = single_cond.shape[1]
    model_width = w_query.shape[1]
    head_count = w_pair.shape[1]
    head_size = model_width // head_count
    seq_place = lax.axis_index("seq")
    sample_place = lax.axis_index("sample")

    bias_local = pair_bias_local(pair_rep, w_pair)
    bias_local, atom_feats = lax.optimization_barrier((bias_local, atom_feats))
    mine = lax.all_to_all(bias_local, "seq", 0, 0, tiled=True)

    relative = (atom_token - seq_place * tok_local)[None, :]
    own, counts, sent = pl.pallas_call(
        atom_kernel,
        out_shape=(
            jax.ShapeDtypeStruct((samp_local, tok_local, model_width), BF16),
            jax.ShapeDtypeStruct((tok_local, 128), F32),
            jax.ShapeDtypeStruct((samp_local, tok_local, model_width + 128), BF16),
        ),
        compiler_params=pltpu.CompilerParams(vmem_limit_bytes=40 * 1024 * 1024),
        cost_estimate=pl.CostEstimate(flops=4 * 10**9, bytes_accessed=3 * 1024 * 1024, transcendentals=0),
    )(atom_feats, relative, w_atom)
    came = from_behind(sent, "seq", 1)
    cond = layer_norm(single_cond.astype(F32)).astype(BF16)
    out_gate = jax.nn.sigmoid(
        jnp.einsum("std,de->ste", cond, w_outgate, preferred_element_type=F32)
        + outgate_bias.astype(F32)
    ).reshape(samp_local * tok_local, model_width)
    gate_ada = jax.nn.sigmoid(jnp.einsum("stc,cd->std", cond, w_ada_gate, preferred_element_type=F32))
    shift_ada = jnp.einsum("stc,cd->std", cond, w_ada_shift, preferred_element_type=F32)
    heads_sent = pl.pallas_call(
        token_kernel,
        out_shape=jax.ShapeDtypeStruct((head_count, 3 * head_size, samp_local * tok_local), BF16),
        compiler_params=pltpu.CompilerParams(vmem_limit_bytes=40 * 1024 * 1024),
        cost_estimate=pl.CostEstimate(flops=3 * 10**9, bytes_accessed=6 * 1024 * 1024, transcendentals=0),
    )(own, counts, came, gate_ada, shift_ada, w_query, w_key, w_value)
    kv = lax.all_to_all(heads_sent, "seq", 0, 0, tiled=True)

    half = mine.shape[0] // 2
    across, up, down = swap_x(mine), shift_y(mine, 1), shift_y(mine, -1)
    far, across_up, across_down = shift_y(up, 1), swap_x(up), shift_y(across, -1)
    across_far = [shift_y(across_up[:half], 1), shift_y(across_down[half:], -1)]
    pieces = [mine, up, down, far, across, across_up, across_down, *across_far]
    pieces = pieces + [swap_core(piece) for piece in pieces]
    x_lo, y, core = sample_place // 8, sample_place // 2 % 4, sample_place % 2
    order = jnp.stack(
        [
            (x_lo ^ dx) * 8 + ((y + dy) % 4) * 2 + (core ^ dc)
            for dc in (0, 1)
            for dx in (0, 1)
            for dy in (0, 3, 1, 2)
        ]
    ).astype(jnp.int32)

    attended = attention(order, kv, pieces)
    attended = lax.all_to_all(attended, "seq", 0, 0, tiled=True).reshape(model_width, -1)
    out = pl.pallas_call(
        finish_kernel,
        out_shape=jax.ShapeDtypeStruct((samp_local * tok_local, model_width), BF16),
        compiler_params=pltpu.CompilerParams(vmem_limit_bytes=40 * 1024 * 1024),
    )(attended, w_out, out_gate)
    return out.reshape(samp_local, tok_local, model_width)


def solution(mesh):
    return jax.shard_map(
        per_device,
        mesh=mesh,
        in_specs=(
            P("sample", "seq", None),
            P("seq"),
            P("sample", "seq", None),
            P("seq", "sample", None),
            P(),
            P(),
            P(),
            P(),
            P(),
            P(),
            P(),
            P(),
            P(),
            P(),
        ),
        out_specs=P("sample", "seq", None),
        check_vma=False,
    )
```

```python
import math

import jax
import jax.numpy as jnp
from jax import lax
from jax.experimental import pallas as pl
from jax.experimental.pallas import tpu as pltpu
from jax.sharding import PartitionSpec as P

F32 = jnp.float32
BF16 = jnp.bfloat16
LOG2E = 1.4426950408889634
ROWS = 256


def from_behind(value, axis, steps):
    count = lax.axis_size(axis)
    initial, last = (max(0, -steps), min(count, count - steps))
    return lax.ppermute(value, axis, [(source, source + steps) for source in range(initial, last)])


def layer_norm(inputs):
    average = jnp.mean(inputs, axis=-1, keepdims=True)
    centered = inputs - average
    variance = jnp.mean(centered * centered, axis=-1, keepdims=True)
    return centered * lax.rsqrt(variance + 1e-05)


def swap_core(value):
    return lax.ppermute(value, "sample", [(i, i ^ 1) for i in range(16)])


def swap_x(value):
    return lax.ppermute(value, "sample", [(i, i ^ 8) for i in range(16)])


def shift_y(value, steps):
    return lax.ppermute(
        value, "sample", [(i, (i & 9) | ((((i >> 1) + steps) & 3) << 1)) for i in range(16)]
    )


def pair_kernel(pair_ref, weight_ref, out_ref, wide_weights, bias_scr):
    step = pl.program_id(0)
    groups, eight, keys, depth = pair_ref.shape
    heads = weight_ref.shape[0]
    width = heads * eight

    @pl.when(step == 0)
    def _():
        lane = lax.broadcasted_iota(jnp.int32, (heads, width), 1)
        row = lax.broadcasted_iota(jnp.int32, (heads, width), 0)
        spread = (lane // eight == row).astype(BF16)
        repeated = lax.dot_general(
            weight_ref[...], spread, (((0,), (0,)), ((), ())), preferred_element_type=F32
        )
        place = lax.broadcasted_iota(jnp.int32, (depth, width), 1) % eight
        for i in range(eight):
            wide_weights[i * depth : (i + 1) * depth, :] = jnp.where(place == i, repeated, 0.0).astype(BF16)

    ones = jnp.ones((depth, depth), BF16)
    normed = []
    for i in range(eight):
        value = pair_ref[:, i].reshape(groups * keys, depth)
        mean = jnp.dot(value, ones, preferred_element_type=F32) * (1.0 / depth)
        centered = value.astype(F32) - mean
        variance = jnp.mean(centered * centered, axis=-1, keepdims=True)
        normed.append((centered * lax.rsqrt(variance + 1e-05)).astype(BF16))
    bias = jnp.dot(jnp.concatenate(normed, axis=1), wide_weights[...], preferred_element_type=F32)
    for group in range(groups):
        turned = bias[group * keys : (group + 1) * keys].T
        for head in range(heads):
            bias_scr[head, pl.ds((step * groups + group) * eight, eight), :] = turned[
                head * eight : (head + 1) * eight
            ]

    @pl.when(step == pl.num_programs(0) - 1)
    def _():
        for head in range(heads):
            out_ref[head] = bias_scr[head].T.astype(BF16)


def pair_bias_local(pair_rep, w_pair, groups=8):
    queries, keys, depth = pair_rep.shape
    heads = w_pair.shape[1]
    eight = 8
    return pl.pallas_call(
        pair_kernel,
        grid=(queries // (eight * groups),),
        in_specs=[
            pl.BlockSpec((groups, eight, keys, depth), lambda i: (i, 0, 0, 0)),
            pl.BlockSpec((heads, depth), lambda i: (0, 0)),
        ],
        out_specs=pl.BlockSpec((heads, keys, queries), lambda i: (0, 0, 0)),
        out_shape=jax.ShapeDtypeStruct((heads, keys, queries), BF16),
        scratch_shapes=[
            pltpu.VMEM((eight * depth, heads * eight), BF16),
            pltpu.VMEM((heads, queries, keys), F32),
        ],
        compiler_params=pltpu.CompilerParams(vmem_limit_bytes=60 * 1024 * 1024),
        cost_estimate=pl.CostEstimate(
            flops=2 * queries * keys * depth * 256, bytes_accessed=5 * 1024 * 1024, transcendentals=queries * keys
        ),
    )(pair_rep.reshape(queries // eight, eight, keys, depth), w_pair.T)


def atom_kernel(feats_ref, relative_ref, weight_ref, own_ref, count_ref, sent_ref):
    samples, atoms, _ = feats_ref.shape
    tok, width = count_ref.shape[0], weight_ref.shape[1]
    slots = lax.broadcasted_iota(jnp.int32, (2 * tok, atoms), 0)
    member = jnp.where(slots == relative_ref[...], 1.0, 0.0)
    counts = jnp.sum(member, axis=1, keepdims=True)
    member = member.astype(BF16)
    count_ref[...] = jnp.broadcast_to(counts[:tok], count_ref.shape)
    above = jnp.broadcast_to(counts[tok:], count_ref.shape)
    high = jnp.floor(above * (1.0 / 256.0)) * 256.0
    lane = lax.broadcasted_iota(jnp.int32, count_ref.shape, 1)
    tail = jnp.where(lane == 0, high, jnp.where(lane == 1, above - high, 0.0)).astype(BF16)
    for sample in range(samples):
        hidden = jnp.dot(feats_ref[sample], weight_ref[...], preferred_element_type=F32)
        hidden = jnp.maximum(hidden, 0.0).astype(BF16)
        partial = jnp.dot(member, hidden, preferred_element_type=F32).astype(BF16)
        own_ref[sample] = partial[:tok]
        sent_ref[sample, :, :width] = partial[tok:]
        sent_ref[sample, :, width:] = tail


def token_kernel(own_ref, count_ref, came_ref, gate_ref, shift_ref, wq_ref, wk_ref, wv_ref, out_ref):
    samples, tok, width = own_ref.shape
    heads, size = out_ref.shape[0], out_ref.shape[1] // 3
    parts = []
    for sample in range(samples):
        tail = came_ref[sample, :, width:].astype(F32)
        count = count_ref[:, 0:1] + tail[:, 0:1] + tail[:, 1:2]
        summed = own_ref[sample].astype(F32) + came_ref[sample, :, :width].astype(F32)
        tokens = summed / count
        average = jnp.mean(tokens, axis=-1, keepdims=True)
        centered = tokens - average
        variance = jnp.mean(centered * centered, axis=-1, keepdims=True)
        normed = centered * lax.rsqrt(variance + 1e-05)
        parts.append((gate_ref[sample] * normed + shift_ref[sample]).astype(BF16))
    normed = jnp.concatenate(parts, axis=0)
    for kind, weight_ref in enumerate((wq_ref, wk_ref, wv_ref)):
        result = jnp.dot(normed, weight_ref[...], preferred_element_type=F32)
        turned = result.T.astype(BF16)
        for head in range(heads):
            out_ref[head, kind * size : (kind + 1) * size, :] = turned[head * size : (head + 1) * size]


def attention_kernel(sample_ref, kv_ref, *refs):
    count = len(refs) - 11
    pieces = refs[:count]
    out_ref, q_scr, k_scr, v_scr, b_scr, s_even, s_odd, m_even, m_odd, sems, kv_scr = refs[count:]
    scores_scr, top_scr = (s_even, s_odd), (m_even, m_odd)
    blocks, size, width = out_ref.shape
    tok = width // 2
    total = blocks * tok
    per_step = ROWS // tok
    steps = blocks // per_step
    chunk = 2 * tok
    scale = LOG2E / math.sqrt(size)

    def copies(step):
        found = []
        for place in range(blocks):
            first, start = place + place // 4, step * per_step
            if place % 4 == 3:
                found.append((pieces[first + start * 2 // blocks], start % (blocks // 2)))
            else:
                found.append((pieces[first], start))
        return [
            pltpu.make_async_copy(
                piece.at[pl.ds(start, per_step)],
                b_scr.at[place, pl.ds(step * per_step, per_step)],
                sems.at[step, place],
            )
            for place, (piece, start) in enumerate(found)
        ]

    kv_copy = pltpu.make_async_copy(kv_ref, kv_scr, sems.at[steps, 0])
    kv_copy.start()
    for step in range(steps):
        for copy in copies(step):
            copy.start()
    kv_copy.wait()
    mine = sample_ref[0]

    for sample in range(2):
        lanes = slice(sample * tok, (sample + 1) * tok)
        for place in range(blocks):
            shift = (0, 3, 1, 2)[place % 4]
            block = (mine ^ (place // 4 % 2 * 8 + place // 8)) & 9
            block = block + ((mine // 2 + shift) % 4) * 2
            span = slice(place * tok, (place + 1) * tok)
            query = kv_scr[place, :size, lanes].astype(F32) * scale
            high = query.astype(BF16)
            q_scr[sample, :size, span] = high
            q_scr[sample, size:, span] = (query - high.astype(F32)).astype(BF16)
            key = kv_scr[block, size : 2 * size, lanes].astype(F32)
            k_scr[sample, span, :] = jnp.concatenate([key, key], axis=0).T.astype(BF16)
            v_scr[sample, :size, span] = kv_scr[block, 2 * size :, lanes]
            v_scr[sample, size:, span] = jnp.ones((v_scr.shape[1] - size, tok), BF16)

    def score(step, slot):
        held = {}

        def part(c):
            if c == 0:
                for place in range(blocks):
                    pltpu.make_async_copy(
                        pieces[0].at[pl.ds(0, per_step)],
                        b_scr.at[place, pl.ds(step * per_step, per_step)],
                        sems.at[step, place],
                    ).wait()
                column = step * ROWS if isinstance(step, int) else pl.multiple_of(step * ROWS, ROWS)
                held["q"] = [q_scr[sample, :, pl.ds(column, ROWS)] for sample in range(2)]
            span = slice(c * chunk, (c + 1) * chunk)
            bias = jnp.concatenate(
                [
                    jnp.concatenate([b_scr[place, step * per_step + t] for t in range(per_step)], axis=1)
                    for place in range(c * chunk // tok, (c + 1) * chunk // tok)
                ],
                axis=0,
            )
            bias = bias.astype(F32) * LOG2E
            for sample in range(2):
                scores = (
                    jnp.dot(k_scr[sample, span, :], held["q"][sample], preferred_element_type=F32) + bias
                )
                scores_scr[slot][sample, span, :] = scores
                top = scores.reshape(chunk // 8, 8, ROWS)
                while top.shape[0] > 4:
                    half = top.shape[0] // 2
                    top = jnp.maximum(top[:half], top[half:])
                held[sample] = top if c == 0 else jnp.maximum(held[sample], top)
                if c == total // chunk - 1:
                    top_scr[slot][sample] = jnp.max(held[sample], axis=0)

        return [lambda c=c: part(c) for c in range(total // chunk)]

    def weigh(step, slot):
        held = {}

        def part(c):
            span = slice(c * chunk, (c + 1) * chunk)
            for sample in range(2):
                if c == 0:
                    held[sample] = jnp.max(top_scr[slot][sample], axis=0, keepdims=True)
                weights = jnp.exp2(scores_scr[slot][sample, span, :] - held[sample]).astype(BF16)
                mixed = jnp.dot(v_scr[sample, :, span], weights, preferred_element_type=F32)
                mixed = mixed if c == 0 else held[sample, 0] + mixed
                held[sample, 0] = mixed
                if c == total // chunk - 1:
                    result = (mixed[:size] / mixed[size : size + 1]).astype(BF16)
                    for t in range(per_step):
                        out_ref[step * per_step + t, :, sample * tok : (sample + 1) * tok] = result[
                            :, t * tok : (t + 1) * tok
                        ]

        return [lambda c=c: part(c) for c in range(total // chunk)]

    def run(*lists):
        for together in zip(*lists):
            for work in together:
                work()

    run(score(0, 0))

    def body(pair, _):
        run(score(2 * pair + 1, 1), weigh(2 * pair, 0))
        run(score(2 * pair + 2, 0), weigh(2 * pair + 1, 1))
        return 0

    lax.fori_loop(0, steps // 2 - 1, body, 0)
    run(score(steps - 1, 1), weigh(steps - 2, 0))
    run(weigh(steps - 1, 1))


def attention(sample_place, kv, pieces):
    blocks, rows3, width = kv.shape
    size = rows3 // 3
    tok = width // 2
    total = blocks * tok
    any_place = pl.BlockSpec(memory_space=pl.ANY)
    return pl.pallas_call(
        attention_kernel,
        in_specs=[pl.BlockSpec(memory_space=pltpu.SMEM)] + [any_place] * (1 + len(pieces)),
        out_specs=pl.BlockSpec(memory_space=pltpu.VMEM),
        out_shape=jax.ShapeDtypeStruct((blocks, size, width), BF16),
        scratch_shapes=[
            pltpu.VMEM((2, 2 * size, total), BF16),
            pltpu.VMEM((2, total, 2 * size), BF16),
            pltpu.VMEM((2, 64, total), BF16),
            pltpu.VMEM((blocks, blocks, tok, tok), BF16),
            pltpu.VMEM((2, total, ROWS), F32),
            pltpu.VMEM((2, total, ROWS), F32),
            pltpu.VMEM((2, 8, ROWS), F32),
            pltpu.VMEM((2, 8, ROWS), F32),
            pltpu.SemaphoreType.DMA((total // ROWS + 1, blocks)),
            pltpu.VMEM(kv.shape, BF16),
        ],
        compiler_params=pltpu.CompilerParams(vmem_limit_bytes=62 * 1024 * 1024),
        cost_estimate=pl.CostEstimate(
            flops=8 * total * total * 64, bytes_accessed=12 * 1024 * 1024, transcendentals=2 * total * total
        ),
    )(sample_place, kv, *pieces)


def finish_kernel(attended_ref, weight_ref, gate_ref, out_ref):
    mixed = lax.dot_general(
        attended_ref[...], weight_ref[...], (((0,), (0,)), ((), ())), preferred_element_type=F32
    )
    out_ref[...] = (gate_ref[...] * mixed).astype(BF16)


def per_device(
    atom_feats,
    atom_token,
    single_cond,
    pair_rep,
    w_atom,
    w_ada_gate,
    w_ada_shift,
    w_query,
    w_key,
    w_value,
    w_pair,
    w_out,
    w_outgate,
    outgate_bias,
):
    samp_local = atom_feats.shape[0]
    atom_local = atom_feats.shape[1]
    tok_local = single_cond.shape[1]
    model_width = w_query.shape[1]
    head_count = w_pair.shape[1]
    head_size = model_width // head_count
    seq_place = lax.axis_index("seq")
    sample_place = lax.axis_index("sample")

    bias_local = pair_bias_local(pair_rep, w_pair)
    bias_local, atom_feats = lax.optimization_barrier((bias_local, atom_feats))

    relative = (atom_token - seq_place * tok_local)[None, :]
    own, counts, sent = pl.pallas_call(
        atom_kernel,
        out_shape=(
            jax.ShapeDtypeStruct((samp_local, tok_local, model_width), BF16),
            jax.ShapeDtypeStruct((tok_local, 128), F32),
            jax.ShapeDtypeStruct((samp_local, tok_local, model_width + 128), BF16),
        ),
        compiler_params=pltpu.CompilerParams(vmem_limit_bytes=40 * 1024 * 1024),
        cost_estimate=pl.CostEstimate(flops=10**6, bytes_accessed=64 * 1024, transcendentals=0),
    )(atom_feats, relative, w_atom)
    bias_local, sent = lax.optimization_barrier((bias_local, sent))
    came = from_behind(sent, "seq", 1)
    mine = lax.all_to_all(bias_local, "seq", 0, 0, tiled=True)

    cond = layer_norm(single_cond.astype(F32)).astype(BF16)
    out_gate = jax.nn.sigmoid(
        jnp.einsum("std,de->ste", cond, w_outgate, preferred_element_type=F32)
        + outgate_bias.astype(F32)
    ).reshape(samp_local * tok_local, model_width)
    gate_ada = jax.nn.sigmoid(jnp.einsum("stc,cd->std", cond, w_ada_gate, preferred_element_type=F32))
    shift_ada = jnp.einsum("stc,cd->std", cond, w_ada_shift, preferred_element_type=F32)
    heads_sent = pl.pallas_call(
        token_kernel,
        out_shape=jax.ShapeDtypeStruct((head_count, 3 * head_size, samp_local * tok_local), BF16),
        compiler_params=pltpu.CompilerParams(vmem_limit_bytes=40 * 1024 * 1024),
        cost_estimate=pl.CostEstimate(flops=10**6, bytes_accessed=64 * 1024, transcendentals=0),
    )(own, counts, came, gate_ada, shift_ada, w_query, w_key, w_value)
    kv = lax.all_to_all(heads_sent, "seq", 0, 0, tiled=True)

    half = mine.shape[0] // 2
    across, up, down = lax.optimization_barrier((swap_x(mine), shift_y(mine, 1), shift_y(mine, -1)))
    far = (shift_y(up[:half], 1), shift_y(down[half:], -1))
    across_up, across_down = shift_y(across, 1), shift_y(across, -1)
    near = [mine, up, down, across]
    far, other = lax.optimization_barrier((far, [swap_core(piece) for piece in near]))
    across_far = [swap_x(part) for part in far]
    late = [*far, across_up, across_down, *across_far]

    def in_order(close, later):
        return [*close[:3], *later[:2], close[3], *later[2:]]

    pieces = in_order(near, late) + in_order(other, [swap_core(piece) for piece in late])

    attended = attention(sample_place[None], kv, pieces)
    attended = lax.all_to_all(attended, "seq", 0, 0, tiled=True).reshape(model_width, -1)
    out = pl.pallas_call(
        finish_kernel,
        out_shape=jax.ShapeDtypeStruct((samp_local * tok_local, model_width), BF16),
        compiler_params=pltpu.CompilerParams(vmem_limit_bytes=40 * 1024 * 1024),
    )(attended, w_out, out_gate)
    return out.reshape(samp_local, tok_local, model_width)


def solution(mesh):
    return jax.shard_map(
        per_device,
        mesh=mesh,
        in_specs=(
            P("sample", "seq", None),
            P("seq"),
            P("sample", "seq", None),
            P("seq", "sample", None),
            P(),
            P(),
            P(),
            P(),
            P(),
            P(),
            P(),
            P(),
            P(),
            P(),
        ),
        out_specs=P("sample", "seq", None),
        check_vma=False,
    )
```

```python
import math

import jax
import jax.numpy as jnp
from jax import lax
from jax.experimental import pallas as pl
from jax.experimental.pallas import tpu as pltpu
from jax.sharding import PartitionSpec as P

F32 = jnp.float32
BF16 = jnp.bfloat16
LOG2E = 1.4426950408889634
ROWS = 256


def from_behind(value, axis, steps):
    count = lax.axis_size(axis)
    initial, last = (max(0, -steps), min(count, count - steps))
    return lax.ppermute(value, axis, [(source, source + steps) for source in range(initial, last)])


def layer_norm(inputs):
    average = jnp.mean(inputs, axis=-1, keepdims=True)
    centered = inputs - average
    variance = jnp.mean(centered * centered, axis=-1, keepdims=True)
    return centered * lax.rsqrt(variance + 1e-05)


def swap_core(value):
    return lax.ppermute(value, "sample", [(i, i ^ 1) for i in range(16)])


def swap_x(value):
    return lax.ppermute(value, "sample", [(i, i ^ 8) for i in range(16)])


def shift_y(value, steps):
    return lax.ppermute(
        value, "sample", [(i, (i & 9) | ((((i >> 1) + steps) & 3) << 1)) for i in range(16)]
    )


def pair_kernel(pair_ref, weight_ref, out_ref, wide_weights, bias_scr):
    step = pl.program_id(0)
    groups, eight, keys, depth = pair_ref.shape
    heads = weight_ref.shape[0]
    width = heads * eight

    @pl.when(step == 0)
    def _():
        lane = lax.broadcasted_iota(jnp.int32, (heads, width), 1)
        row = lax.broadcasted_iota(jnp.int32, (heads, width), 0)
        spread = (lane // eight == row).astype(BF16)
        repeated = lax.dot_general(
            weight_ref[...], spread, (((0,), (0,)), ((), ())), preferred_element_type=F32
        )
        place = lax.broadcasted_iota(jnp.int32, (depth, width), 1) % eight
        for i in range(eight):
            wide_weights[i * depth : (i + 1) * depth, :] = jnp.where(place == i, repeated, 0.0).astype(BF16)

    ones = jnp.ones((depth, depth), BF16)
    normed = []
    for i in range(eight):
        value = pair_ref[:, i].reshape(groups * keys, depth)
        mean = jnp.dot(value, ones, preferred_element_type=F32) * (1.0 / depth)
        centered = value.astype(F32) - mean
        variance = jnp.mean(centered * centered, axis=-1, keepdims=True)
        normed.append((centered * lax.rsqrt(variance + 1e-05)).astype(BF16))
    bias = jnp.dot(jnp.concatenate(normed, axis=1), wide_weights[...], preferred_element_type=F32)
    for group in range(groups):
        turned = bias[group * keys : (group + 1) * keys].T
        for head in range(heads):
            bias_scr[head, pl.ds((step * groups + group) * eight, eight), :] = turned[
                head * eight : (head + 1) * eight
            ]

    @pl.when(step == pl.num_programs(0) - 1)
    def _():
        for head in range(heads):
            out_ref[head] = bias_scr[head].T.astype(BF16)


def pair_bias_local(pair_rep, w_pair, groups=8):
    queries, keys, depth = pair_rep.shape
    heads = w_pair.shape[1]
    eight = 8
    return pl.pallas_call(
        pair_kernel,
        grid=(queries // (eight * groups),),
        in_specs=[
            pl.BlockSpec((groups, eight, keys, depth), lambda i: (i, 0, 0, 0)),
            pl.BlockSpec((heads, depth), lambda i: (0, 0)),
        ],
        out_specs=pl.BlockSpec((heads, keys, queries), lambda i: (0, 0, 0)),
        out_shape=jax.ShapeDtypeStruct((heads, keys, queries), BF16),
        scratch_shapes=[
            pltpu.VMEM((eight * depth, heads * eight), BF16),
            pltpu.VMEM((heads, queries, keys), F32),
        ],
        compiler_params=pltpu.CompilerParams(vmem_limit_bytes=60 * 1024 * 1024),
        cost_estimate=pl.CostEstimate(
            flops=2 * queries * keys * depth * 256, bytes_accessed=5 * 1024 * 1024, transcendentals=queries * keys
        ),
    )(pair_rep.reshape(queries // eight, eight, keys, depth), w_pair.T)


def atom_kernel(feats_ref, relative_ref, weight_ref, own_ref, count_ref, sent_ref):
    samples, atoms, _ = feats_ref.shape
    tok, width = count_ref.shape[0], weight_ref.shape[1]
    slots = lax.broadcasted_iota(jnp.int32, (2 * tok, atoms), 0)
    member = jnp.where(slots == relative_ref[...], 1.0, 0.0)
    counts = jnp.sum(member, axis=1, keepdims=True)
    member = member.astype(BF16)
    count_ref[...] = jnp.broadcast_to(counts[:tok], count_ref.shape)
    above = jnp.broadcast_to(counts[tok:], count_ref.shape)
    high = jnp.floor(above * (1.0 / 256.0)) * 256.0
    lane = lax.broadcasted_iota(jnp.int32, count_ref.shape, 1)
    tail = jnp.where(lane == 0, high, jnp.where(lane == 1, above - high, 0.0)).astype(BF16)
    for sample in range(samples):
        hidden = jnp.dot(feats_ref[sample], weight_ref[...], preferred_element_type=F32)
        hidden = jnp.maximum(hidden, 0.0).astype(BF16)
        partial = jnp.dot(member, hidden, preferred_element_type=F32).astype(BF16)
        own_ref[sample] = partial[:tok]
        sent_ref[sample, :, :width] = partial[tok:]
        sent_ref[sample, :, width:] = tail


def token_kernel(own_ref, count_ref, came_ref, gate_ref, shift_ref, wq_ref, wk_ref, wv_ref, out_ref):
    samples, tok, width = own_ref.shape
    heads, size = out_ref.shape[0], out_ref.shape[1] // 3
    parts = []
    for sample in range(samples):
        tail = came_ref[sample, :, width:].astype(F32)
        count = count_ref[:, 0:1] + tail[:, 0:1] + tail[:, 1:2]
        summed = own_ref[sample].astype(F32) + came_ref[sample, :, :width].astype(F32)
        tokens = summed / count
        average = jnp.mean(tokens, axis=-1, keepdims=True)
        centered = tokens - average
        variance = jnp.mean(centered * centered, axis=-1, keepdims=True)
        normed = centered * lax.rsqrt(variance + 1e-05)
        parts.append((gate_ref[sample] * normed + shift_ref[sample]).astype(BF16))
    normed = jnp.concatenate(parts, axis=0)
    for kind, weight_ref in enumerate((wq_ref, wk_ref, wv_ref)):
        result = jnp.dot(normed, weight_ref[...], preferred_element_type=F32)
        turned = result.T.astype(BF16)
        for head in range(heads):
            out_ref[head, kind * size : (kind + 1) * size, :] = turned[head * size : (head + 1) * size]


def attention_kernel(sample_ref, kv_ref, *refs):
    count = len(refs) - 11
    pieces = refs[:count]
    out_ref, q_scr, k_scr, v_scr, b_scr, s_even, s_odd, m_even, m_odd, sems, kv_scr = refs[count:]
    scores_scr, top_scr = (s_even, s_odd), (m_even, m_odd)
    blocks, size, width = out_ref.shape
    tok = width // 2
    total = blocks * tok
    per_step = ROWS // tok
    steps = blocks // per_step
    chunk = 2 * tok
    scale = LOG2E / math.sqrt(size)

    def copies(step):
        found = [(piece, step * per_step) for piece in pieces]
        return [
            pltpu.make_async_copy(
                piece.at[pl.ds(start, per_step)],
                b_scr.at[place, pl.ds(step * per_step, per_step)],
                sems.at[step, place],
            )
            for place, (piece, start) in enumerate(found)
        ]

    kv_copy = pltpu.make_async_copy(kv_ref, kv_scr, sems.at[steps, 0])
    kv_copy.start()
    for step in range(steps):
        for copy in copies(step):
            copy.start()
    kv_copy.wait()
    mine = sample_ref[0]

    for sample in range(2):
        lanes = slice(sample * tok, (sample + 1) * tok)
        for place in range(blocks):
            shift = (0, 3, 1, 2)[place % 4]
            block = (mine ^ (place // 4 % 2 * 8 + place // 8)) & 9
            block = block + ((mine // 2 + shift) % 4) * 2
            span = slice(place * tok, (place + 1) * tok)
            query = kv_scr[place, :size, lanes].astype(F32) * scale
            high = query.astype(BF16)
            q_scr[sample, :size, span] = high
            q_scr[sample, size:, span] = (query - high.astype(F32)).astype(BF16)
            key = kv_scr[block, size : 2 * size, lanes].astype(F32)
            k_scr[sample, span, :] = jnp.concatenate([key, key], axis=0).T.astype(BF16)
            v_scr[sample, :size, span] = kv_scr[block, 2 * size :, lanes]
            v_scr[sample, size:, span] = jnp.ones((v_scr.shape[1] - size, tok), BF16)

    def score(step, slot):
        held = {}

        def part(c):
            if c == 0:
                for place in range(blocks):
                    pltpu.make_async_copy(
                        pieces[0].at[pl.ds(0, per_step)],
                        b_scr.at[place, pl.ds(step * per_step, per_step)],
                        sems.at[step, place],
                    ).wait()
                column = step * ROWS if isinstance(step, int) else pl.multiple_of(step * ROWS, ROWS)
                held["q"] = [q_scr[sample, :, pl.ds(column, ROWS)] for sample in range(2)]
            span = slice(c * chunk, (c + 1) * chunk)
            bias = jnp.concatenate(
                [
                    jnp.concatenate([b_scr[place, step * per_step + t] for t in range(per_step)], axis=1)
                    for place in range(c * chunk // tok, (c + 1) * chunk // tok)
                ],
                axis=0,
            )
            bias = bias.astype(F32) * LOG2E
            for sample in range(2):
                scores = (
                    jnp.dot(k_scr[sample, span, :], held["q"][sample], preferred_element_type=F32) + bias
                )
                scores_scr[slot][sample, span, :] = scores
                top = scores.reshape(chunk // 8, 8, ROWS)
                while top.shape[0] > 4:
                    half = top.shape[0] // 2
                    top = jnp.maximum(top[:half], top[half:])
                held[sample] = top if c == 0 else jnp.maximum(held[sample], top)
                if c == total // chunk - 1:
                    top_scr[slot][sample] = jnp.max(held[sample], axis=0)

        return [lambda c=c: part(c) for c in range(total // chunk)]

    def weigh(step, slot):
        held = {}

        def part(c):
            span = slice(c * chunk, (c + 1) * chunk)
            for sample in range(2):
                if c == 0:
                    held[sample] = jnp.max(top_scr[slot][sample], axis=0, keepdims=True)
                weights = jnp.exp2(scores_scr[slot][sample, span, :] - held[sample]).astype(BF16)
                mixed = jnp.dot(v_scr[sample, :, span], weights, preferred_element_type=F32)
                mixed = mixed if c == 0 else held[sample, 0] + mixed
                held[sample, 0] = mixed
                if c == total // chunk - 1:
                    result = (mixed[:size] / mixed[size : size + 1]).astype(BF16)
                    for t in range(per_step):
                        out_ref[step * per_step + t, :, sample * tok : (sample + 1) * tok] = result[
                            :, t * tok : (t + 1) * tok
                        ]

        return [lambda c=c: part(c) for c in range(total // chunk)]

    def run(*lists):
        for together in zip(*lists):
            for work in together:
                work()

    run(score(0, 0))

    def body(pair, _):
        run(score(2 * pair + 1, 1), weigh(2 * pair, 0))
        run(score(2 * pair + 2, 0), weigh(2 * pair + 1, 1))
        return 0

    lax.fori_loop(0, steps // 2 - 1, body, 0)
    run(score(steps - 1, 1), weigh(steps - 2, 0))
    run(weigh(steps - 1, 1))


def attention(sample_place, kv, pieces):
    blocks, rows3, width = kv.shape
    size = rows3 // 3
    tok = width // 2
    total = blocks * tok
    any_place = pl.BlockSpec(memory_space=pl.ANY)
    return pl.pallas_call(
        attention_kernel,
        in_specs=[pl.BlockSpec(memory_space=pltpu.SMEM)] + [any_place] * (1 + len(pieces)),
        out_specs=pl.BlockSpec(memory_space=pltpu.VMEM),
        out_shape=jax.ShapeDtypeStruct((blocks, size, width), BF16),
        scratch_shapes=[
            pltpu.VMEM((2, 2 * size, total), BF16),
            pltpu.VMEM((2, total, 2 * size), BF16),
            pltpu.VMEM((2, 64, total), BF16),
            pltpu.VMEM((blocks, blocks, tok, tok), BF16),
            pltpu.VMEM((2, total, ROWS), F32),
            pltpu.VMEM((2, total, ROWS), F32),
            pltpu.VMEM((2, 8, ROWS), F32),
            pltpu.VMEM((2, 8, ROWS), F32),
            pltpu.SemaphoreType.DMA((total // ROWS + 1, blocks)),
            pltpu.VMEM(kv.shape, BF16),
        ],
        compiler_params=pltpu.CompilerParams(vmem_limit_bytes=62 * 1024 * 1024),
        cost_estimate=pl.CostEstimate(
            flops=8 * total * total * 64, bytes_accessed=12 * 1024 * 1024, transcendentals=2 * total * total
        ),
    )(sample_place, kv, *pieces)


def finish_kernel(attended_ref, weight_ref, gate_ref, out_ref):
    mixed = lax.dot_general(
        attended_ref[...], weight_ref[...], (((0,), (0,)), ((), ())), preferred_element_type=F32
    )
    out_ref[...] = (gate_ref[...] * mixed).astype(BF16)


def per_device(
    atom_feats,
    atom_token,
    single_cond,
    pair_rep,
    w_atom,
    w_ada_gate,
    w_ada_shift,
    w_query,
    w_key,
    w_value,
    w_pair,
    w_out,
    w_outgate,
    outgate_bias,
):
    samp_local = atom_feats.shape[0]
    atom_local = atom_feats.shape[1]
    tok_local = single_cond.shape[1]
    model_width = w_query.shape[1]
    head_count = w_pair.shape[1]
    head_size = model_width // head_count
    seq_place = lax.axis_index("seq")
    sample_place = lax.axis_index("sample")

    bias_local = pair_bias_local(pair_rep, w_pair)
    bias_local, atom_feats = lax.optimization_barrier((bias_local, atom_feats))

    relative = (atom_token - seq_place * tok_local)[None, :]
    own, counts, sent = pl.pallas_call(
        atom_kernel,
        out_shape=(
            jax.ShapeDtypeStruct((samp_local, tok_local, model_width), BF16),
            jax.ShapeDtypeStruct((tok_local, 128), F32),
            jax.ShapeDtypeStruct((samp_local, tok_local, model_width + 128), BF16),
        ),
        compiler_params=pltpu.CompilerParams(vmem_limit_bytes=40 * 1024 * 1024),
        cost_estimate=pl.CostEstimate(flops=10**6, bytes_accessed=64 * 1024, transcendentals=0),
    )(atom_feats, relative, w_atom)
    bias_local, sent = lax.optimization_barrier((bias_local, sent))
    came = from_behind(sent, "seq", 1)
    mine = lax.all_to_all(bias_local, "seq", 0, 0, tiled=True)

    cond = layer_norm(single_cond.astype(F32)).astype(BF16)
    out_gate = jax.nn.sigmoid(
        jnp.einsum("std,de->ste", cond, w_outgate, preferred_element_type=F32)
        + outgate_bias.astype(F32)
    ).reshape(samp_local * tok_local, model_width)
    gate_ada = jax.nn.sigmoid(jnp.einsum("stc,cd->std", cond, w_ada_gate, preferred_element_type=F32))
    shift_ada = jnp.einsum("stc,cd->std", cond, w_ada_shift, preferred_element_type=F32)
    heads_sent = pl.pallas_call(
        token_kernel,
        out_shape=jax.ShapeDtypeStruct((head_count, 3 * head_size, samp_local * tok_local), BF16),
        compiler_params=pltpu.CompilerParams(vmem_limit_bytes=40 * 1024 * 1024),
        cost_estimate=pl.CostEstimate(flops=10**6, bytes_accessed=64 * 1024, transcendentals=0),
    )(own, counts, came, gate_ada, shift_ada, w_query, w_key, w_value)
    kv = lax.all_to_all(heads_sent, "seq", 0, 0, tiled=True)

    half = mine.shape[0] // 2
    across, up, down = lax.optimization_barrier((swap_x(mine), shift_y(mine, 1), shift_y(mine, -1)))
    far = (shift_y(up[:half], 1), shift_y(down[half:], -1))
    across_up, across_down = shift_y(across, 1), shift_y(across, -1)
    near = [mine, up, down, across]
    far, other = lax.optimization_barrier((far, [swap_core(piece) for piece in near]))
    far = jnp.concatenate(far, axis=0)
    late = [far, across_up, across_down, swap_x(far)]

    def in_order(close, later):
        return [*close[:3], later[0], close[3], *later[1:]]

    pieces = in_order(near, late) + in_order(other, [swap_core(piece) for piece in late])

    attended = attention(sample_place[None], kv, pieces)
    attended = lax.all_to_all(attended, "seq", 0, 0, tiled=True).reshape(model_width, -1)
    out = pl.pallas_call(
        finish_kernel,
        out_shape=jax.ShapeDtypeStruct((samp_local * tok_local, model_width), BF16),
        compiler_params=pltpu.CompilerParams(vmem_limit_bytes=40 * 1024 * 1024),
    )(attended, w_out, out_gate)
    return out.reshape(samp_local, tok_local, model_width)


def solution(mesh):
    return jax.shard_map(
        per_device,
        mesh=mesh,
        in_specs=(
            P("sample", "seq", None),
            P("seq"),
            P("sample", "seq", None),
            P("seq", "sample", None),
            P(),
            P(),
            P(),
            P(),
            P(),
            P(),
            P(),
            P(),
            P(),
            P(),
        ),
        out_specs=P("sample", "seq", None),
        check_vma=False,
    )
```
